32 devices in a mesh: ens: 4 (over y, x), space: 8 (over z, core).
Axes of the slice: x: 2, y: 2, z: 4, core: 2. Of those that a mesh axis runs over, the one named last changes fastest.
Arguments:
- node_latent: bfloat16 [4, 2048, 512], P('ens', 'space'), may hold values from -6 to 6
- point_skip: bfloat16 [16384, 512], P('space'), may hold values from -6 to 6
- edge_index: int32 [3, 16384], P(None, 'space'), may hold values from 0 to 319
- edge_weight: float32 [3, 16384], P(None, 'space'), may hold values from 0.1 to 1
- w_in: bfloat16 [512, 512], replicated, may hold values from -0.25 to 0.25
- b_in: float32 [512], replicated, may hold values from -3 to 3
- readout_matrix: bfloat16 [10, 512], replicated, may hold values from -0.25 to 0.25
- output_bias: float32 [10], replicated, may hold values from -3 to 3
- truth: float32 [10, 16384], P(None, 'space'), may hold values from -6 to 6
Outputs:
- loss: float32 [], replicated
- grad_latent: float32 [4, 2048, 512], P('ens', 'space')
- grad_w_in: float32 [512, 512], replicated
- grad_b_in: float32 [512], replicated
- grad_w_out: float32 [10, 512], replicated
- grad_b_out: float32 [10], replicated
The draws below stay inside these ranges and needn't reach their ends.
Inputs may be any that keep to these rules, and one draw needn't show every extreme that they name: edge_index[k, p] indexes the table of 320 mesh nodes of p's band: the last 32 nodes of the band before, the band's own 256, the first 32 of the band after.
All inputs are finite; a program needn't handle non-finite values.
Results may differ from the reference program's by a relative error of at most 0.019.
The reference program's roundings to bfloat16 on the way count: a program that leaves them out, or rounds other values in their place, can miss the bound.
Values may be sent and summed in bfloat16 or wider, within the bound.
A program may use at most 64 MiB of HBM per device.

```python
import math
import jax
import jax.numpy as jnp
from jax import lax

C = 512
H = 512
V = 10
K = 3
PTS_DEV = 2048
NODE_DEV = 256
R = 32
TOTAL_MEMBERS_N = 4
POINTS = 16384
NODES = 2048
N_SPACE = 8


def set_ends(drawn, rng, smallest, top_value):
    longest = drawn.shape.index(max(drawn.shape))
    spots = []
    for shift in (0, 1):
        where = [jax.random.randint(jax.random.fold_in(rng, axis), (), 0, length) for axis, length in enumerate(drawn.shape)]
        where[longest] = (where[longest] + shift) % drawn.shape[longest]
        spots.append(tuple(where))
    return drawn.at[spots[0]].set(smallest).at[spots[1]].set(top_value)


def shard_levels(rng, extent, shards, smallest, largest):
    level = 1.0
    for position, shards_of in shards:
        heights = jax.random.uniform(jax.random.fold_in(jax.random.fold_in(rng, 6), position), (shards_of,), jnp.float32, smallest / len(shards), largest / len(shards))
        level = level * jnp.repeat(jnp.exp(heights), extent[position] // shards_of).reshape((-1,) + (1,) * (len(extent) - 1 - position))
    return level


def noise(own_key, shape, scale, bound, shards=(), held_as=jnp.bfloat16):
    drawn = scale * jax.random.normal(own_key, shape, jnp.float32)
    if shards:
        drawn = drawn * shard_levels(own_key, shape, shards, -0.22, 0.18)
    return jnp.clip(drawn, -bound, bound).astype(held_as)


def setup_inputs(seed: int = 0) -> dict:
    splits = jax.random.split(jax.random.key(seed), 10)
    node_latent = noise(splits[0], (TOTAL_MEMBERS_N, NODES, C), 1.0, 6.0, ((0, 4), (1, 8)))
    point_skip = noise(splits[1], (POINTS, C), 1.0, 6.0, ((0, 8),))
    edge_index = set_ends(jax.random.randint(splits[2], (K, POINTS), 0, NODE_DEV + 2 * R), jax.random.fold_in(splits[2], 1), 0, (NODE_DEV + 2 * R) - 1).astype(jnp.int32)
    edge_weight = jnp.clip(jnp.exp(math.log(1.0) - 2.3025851 * jax.random.uniform(splits[3], (K, POINTS), jnp.float32) ** shard_levels(splits[3], (K, POINTS), ((1, 8),), -0.2, 0.2)), 0.1, 1.0)
    w_in = noise(splits[4], (C, H), C ** -0.5, 0.25)
    b_in = noise(splits[5], (H,), 0.5, 3.0, (), jnp.float32)
    readout_matrix = noise(splits[6], (V, H), H ** -0.5, 0.25)
    output_bias = noise(splits[7], (V,), 0.5, 3.0, (), jnp.float32)
    truth = noise(splits[8], (V, POINTS), 1.0, 6.0, ((1, 8),), jnp.float32)
    return dict(node_latent=node_latent, point_skip=point_skip, edge_index=edge_index, edge_weight=edge_weight, w_in=w_in, b_in=b_in, readout_matrix=readout_matrix, output_bias=output_bias, truth=truth)


unbiasing_factor = 0.95

def mutual_gaps_between_draws(owned_entries_window, all_members, verifying_truth_state, per_draw_states):
    spread_among_draws = owned_entries_window[:, None] - all_members[None]
    predicted_state_adjoint = jnp.sign(owned_entries_window - verifying_truth_state[None]) / per_draw_states - unbiasing_factor / (per_draw_states * (per_draw_states - 1)) * lax.optimization_barrier(jnp.sum(jnp.sign(spread_among_draws), axis=1))
    accumulated_total_so_far = jnp.sum(jnp.abs(owned_entries_window - verifying_truth_state[None])) / per_draw_states - unbiasing_factor / (2.0 * per_draw_states * (per_draw_states - 1)) * jnp.sum(jnp.abs(spread_among_draws))
    return (predicted_state_adjoint, accumulated_total_so_far)

def reference(node_latent, point_skip, edge_index, edge_weight, w_in, b_in, readout_matrix, output_bias, truth):
    padded = jnp.pad(node_latent, ((0, 0), (R, R), (0, 0)))
    adjoint_multiplier = 1.0 / math.sqrt(TOTAL_MEMBERS_N * POINTS)
    table_len = NODE_DEV + 2 * R

    def band_step(carry, band):
        node_grad, gw_in, gb_in, readout_matrix_adjoint, readout_offset_adjoint, loss_sum = carry
        node_start = band * NODE_DEV
        extended = lax.dynamic_slice_in_dim(padded, node_start, table_len, 1)
        start = band * PTS_DEV
        skip_band = lax.dynamic_slice_in_dim(point_skip, start, PTS_DEV, 0)
        index_band = lax.dynamic_slice_in_dim(edge_index, start, PTS_DEV, 1)
        weight_band = lax.dynamic_slice_in_dim(edge_weight, start, PTS_DEV, 1)
        verifying_truth_state = lax.dynamic_slice_in_dim(truth, start, PTS_DEV, 1)
        gathered_sum = jnp.broadcast_to(skip_band.astype(jnp.float32)[None], (TOTAL_MEMBERS_N, PTS_DEV, C))
        for edge in range(K):
            gathered_sum = gathered_sum + weight_band[edge][None, :, None] * extended[:, index_band[edge], :].astype(jnp.float32)
        features = gathered_sum.astype(jnp.bfloat16)
        preact = jnp.einsum('mpc,ch->mph', features.astype(jnp.float32), w_in.astype(jnp.float32)) + b_in
        inner_layer_response = jax.nn.silu(preact).astype(jnp.bfloat16)
        modelled_state_values = jnp.einsum('rfo,to->rtf', inner_layer_response.astype(jnp.float32), readout_matrix.astype(jnp.float32)) + output_bias[None, :, None]
        predicted_state_adjoint, accumulated_total_so_far = mutual_gaps_between_draws(modelled_state_values, modelled_state_values, verifying_truth_state, TOTAL_MEMBERS_N)
        readout_offset_adjoint = readout_offset_adjoint + lax.optimization_barrier(jnp.sum(predicted_state_adjoint, axis=(0, 2)))
        readout_matrix_adjoint = readout_matrix_adjoint + jnp.einsum('vsp,vpr->sr', predicted_state_adjoint, inner_layer_response.astype(jnp.float32), precision=lax.Precision.HIGHEST)
        inner_layer_adjoint = jnp.einsum('hqs,qi->hsi', predicted_state_adjoint, readout_matrix.astype(jnp.float32), precision=lax.Precision.HIGHEST)
        sigmoid_pre = jax.nn.sigmoid(preact)
        d_preact = (inner_layer_adjoint * sigmoid_pre * (1.0 + preact * (1.0 - sigmoid_pre))).astype(jnp.bfloat16)
        gb_in = gb_in + lax.optimization_barrier(jnp.sum(d_preact.astype(jnp.float32), axis=(0, 1)))
        gw_in = gw_in + jnp.einsum('mpc,mph->ch', features.astype(jnp.float32), d_preact.astype(jnp.float32))
        d_features = jnp.einsum('mph,ch->mpc', d_preact.astype(jnp.float32), w_in.astype(jnp.float32))
        local_grad = jnp.zeros((TOTAL_MEMBERS_N, table_len, C), jnp.float32)
        for edge in range(K):
            local_grad = local_grad.at[:, index_band[edge], :].add(weight_band[edge][None, :, None] * d_features)
        window = lax.dynamic_slice_in_dim(node_grad, node_start, table_len, 1)
        node_grad = lax.dynamic_update_slice_in_dim(node_grad, window + local_grad, node_start, 1)
        return ((node_grad, gw_in, gb_in, readout_matrix_adjoint, readout_offset_adjoint, loss_sum + accumulated_total_so_far), None)
    init = (jnp.zeros((TOTAL_MEMBERS_N, NODES + 2 * R, C), jnp.float32), jnp.zeros((C, H), jnp.float32), jnp.zeros((H,), jnp.float32), jnp.zeros((V, H), jnp.float32), jnp.zeros((V,), jnp.float32), jnp.zeros((), jnp.float32))
    final, _ = lax.scan(band_step, init, jnp.arange(N_SPACE, dtype=jnp.int32))
    node_grad, gw_in, gb_in, readout_matrix_adjoint, readout_offset_adjoint, loss_sum = final
    loss = loss_sum / (POINTS * V)
    grad_latent = node_grad[:, R:R + NODES, :]
    return (loss, grad_latent, gw_in * adjoint_multiplier, gb_in * adjoint_multiplier, readout_matrix_adjoint * adjoint_multiplier, readout_offset_adjoint * adjoint_multiplier)
```

```python
import functools
import math

import jax
import jax.numpy as jnp
from jax import lax
from jax.experimental import pallas as pl
from jax.experimental.pallas import tpu as pltpu
from jax.sharding import PartitionSpec as P

UNBIASING = 0.95
F32 = jnp.float32
BF16 = jnp.bfloat16
NT = (((1,), (1,)), ((), ()))


def dot(a, b):
    return jnp.dot(a, b, preferred_element_type=F32)


def dot_nt(a, b):
    return lax.dot_general(a, b, NT, preferred_element_type=F32)


def sign(x):
    return jnp.where(x > 0, 1.0, 0.0) - jnp.where(x < 0, 1.0, 0.0)


def kernel(
    cfg,
    latent, skip_hbm, index, weight, w_in, b_in, readout, bias, truth,
    node_out, gw_out_ref, small_out,
    skip, ext, ext_t, table, w_t, feat, hid, slope, dpre, fc, fc_in,
    ro_pad, truth_pad, b_col, acc_bin, acc_bout, acc_loss, node_grad,
    rim_send, rim_recv, gw_send, sum_a, recv_a, send_b, sum_b, recv_b, send_c, recv_c, gout,
    small, small_a, small_b, small_c,
    local_sem, halo_s, halo_r, fc_s, fc_r, rim_s, rim_r, a_s, a_r, b_s, b_r, c_s, c_r,
    gc_s, gc_r, gb_s, gb_r, ga_s, ga_r, sa_s, sa_r, sb_s, sb_r, sc_s, sc_r,
):
    E, S, T, R = cfg
    Z = S // 2
    nodes, C = latent.shape
    H = w_in.shape[1]
    pts = skip.shape[0]
    K = index.shape[0]
    V = readout.shape[0]
    VP = ro_pad.shape[0]
    tiles = pts // T
    table_len = nodes + 2 * R
    e = lax.axis_index("ens")
    s = lax.axis_index("space")
    c = lax.rem(s, 2)
    z = lax.div(s, 2)
    partner = s + 1 - 2 * c
    far = s - 1 + 2 * c
    has_far = jnp.logical_and(far >= 0, far < S)

    skip_copy = pltpu.make_async_copy(skip_hbm, skip, local_sem)
    skip_copy.start()

    barrier = pltpu.get_barrier_semaphore()

    def greet(dev):
        pl.semaphore_signal(barrier, inc=1, device_id=dev, device_id_type=pl.DeviceIdType.MESH)

    def ens_peer(d):
        return lax.rem(e + d, E)

    def z_peer(d):
        return lax.rem(z + d, Z)

    greet((e, partner))
    for d in range(1, E):
        greet((ens_peer(d), s))
    for d in range(1, Z):
        greet((e, 2 * z_peer(d) + c))

    @pl.when(has_far)
    def _():
        greet((e, far))

    pl.semaphore_wait(barrier, E + Z - 1 + has_far.astype(jnp.int32))

    def remote(src, dst, ss, rs, dev):
        return pltpu.make_async_remote_copy(
            src_ref=src, dst_ref=dst, send_sem=ss, recv_sem=rs,
            device_id=dev, device_id_type=pl.DeviceIdType.MESH,
        )

    up = remote(latent.at[pl.ds(nodes - R, R)], ext.at[pl.ds(0, R)], halo_s.at[0], halo_r.at[0], (e, s + 1))
    down = remote(latent.at[pl.ds(0, R)], ext.at[pl.ds(R + nodes, R)], halo_s.at[1], halo_r.at[1], (e, s - 1))

    @pl.when(s < S - 1)
    def _():
        up.start()

    @pl.when(s > 0)
    def _():
        down.start()

    @pl.when(s == 0)
    def _():
        ext[pl.ds(0, R)] = jnp.zeros((R, C), BF16)

    @pl.when(s == S - 1)
    def _():
        ext[pl.ds(R + nodes, R)] = jnp.zeros((R, C), BF16)

    ext[pl.ds(R, nodes)] = latent[...]
    ext[pl.ds(table_len + R, nodes)] = latent[...]
    w_t[...] = jnp.transpose(w_in[...])
    b_col[...] = jnp.transpose(jnp.broadcast_to(b_in[...], (128, H)))
    ro_pad[...] = jnp.zeros_like(ro_pad)
    ro_pad[pl.ds(0, V)] = readout[...].astype(F32)
    truth_pad[...] = jnp.zeros_like(truth_pad)
    truth_pad[pl.ds(0, V)] = truth[...]
    acc_bin[...] = jnp.zeros_like(acc_bin)
    acc_bout[...] = jnp.zeros_like(acc_bout)
    acc_loss[...] = jnp.zeros_like(acc_loss)
    small[...] = jnp.zeros_like(small)
    ro = ro_pad[...].astype(BF16)
    ro_t = jnp.transpose(ro_pad[...]).astype(BF16)
    row_v = lax.broadcasted_iota(jnp.int32, (VP, 128), 0)
    lane_v = lax.broadcasted_iota(jnp.int32, (VP, 128), 1)
    bias_col = jnp.sum(
        jnp.where(row_v == lane_v, jnp.broadcast_to(bias[...], (VP, 128)), 0.0), axis=1, keepdims=True
    )

    def lanes(i):
        return pl.ds(pl.multiple_of(i * T, T), T)

    def make_table(i, carry):
        slot = lax.broadcasted_iota(jnp.int32, (table_len, T), 0)
        total = jnp.zeros((table_len, T), F32)
        for k in range(K):
            total = total + jnp.where(slot == index[pl.ds(k, 1), lanes(i)], weight[pl.ds(k, 1), lanes(i)], 0.0)
        high = total.astype(BF16)
        table[pl.ds(0, table_len), lanes(i)] = high
        table[pl.ds(table_len, table_len), lanes(i)] = (total - high.astype(F32)).astype(BF16)
        return carry

    lax.fori_loop(0, tiles, make_table, 0)
    skip_copy.wait()

    @pl.when(s < S - 1)
    def _():
        down.wait_recv()

    @pl.when(s > 0)
    def _():
        up.wait_recv()

    ext[pl.ds(table_len, R)] = ext[pl.ds(0, R)]
    ext[pl.ds(table_len + R + nodes, R)] = ext[pl.ds(R + nodes, R)]
    ext_t[...] = jnp.transpose(ext[...])

    units = 20.0 * E * (E - 1)
    from_truth = 20.0 * (E - 1)
    from_pair = 20.0 * UNBIASING

    def fc_copy(i, d):
        return remote(fc.at[i], fc_in.at[i, d - 1], fc_s.at[i, d - 1], fc_r.at[i, d - 1], (ens_peer(d), s))

    def forward(i, carry):
        at = lanes(i)
        skip_t = jnp.transpose(skip[at, :]).astype(F32)
        f = (skip_t + dot(ext_t[...], table[:, at])).astype(BF16)
        feat[:, at] = f
        col = b_col[...]
        pre = dot(w_t[...], f) + jnp.concatenate([col] * (T // 128), axis=1)
        sig = 1.0 / (1.0 + jnp.exp(-pre))
        h = pre * sig
        slope[:, at] = (sig + h * (1.0 - sig)) * (1.0 / units)
        hb = h.astype(BF16)
        hid[:, at] = hb
        fc[i] = (dot(ro, hb) + bias_col)[:V]
        for d in range(1, E):
            fc_copy(i, d).start()
        return carry

    lax.fori_loop(0, tiles, forward, 0)

    def backward(i, carry):
        at = lanes(i)
        for d in range(1, E):
            fc_copy(i, d).wait_recv()
        own = fc[i]
        gap = own - truth_pad[pl.ds(0, V), at]
        pairs = jnp.zeros_like(own)
        spread = jnp.zeros_like(own)
        for d in range(1, E):
            diff = own - fc_in[i, d - 1]
            pairs = pairs + sign(diff)
            spread = spread + jnp.abs(diff)
        adj = from_truth * sign(gap) - from_pair * pairs
        acc_bout[pl.ds(0, V)] += adj
        acc_loss[pl.ds(0, V)] += jnp.abs(gap) * (1.0 / E) - spread * (UNBIASING / (2.0 * E * (E - 1)))
        truth_pad[pl.ds(0, V), at] = adj
        g = truth_pad[:, at].astype(BF16)
        small[...] += dot_nt(g, hid[:, at])
        dp = (dot(ro_t, g) * slope[:, at]).astype(BF16)
        dpre[:, at] = dp
        dp32 = dp.astype(F32)
        part = dp32[:, 0:128]
        for j in range(1, T // 128):
            part = part + dp32[:, j * 128:(j + 1) * 128]
        acc_bin[...] += part
        return carry

    lax.fori_loop(0, tiles, backward, 0)

    row = lax.broadcasted_iota(jnp.int32, (VP, H), 0)
    lane = lax.broadcasted_iota(jnp.int32, (VP, H), 1)
    gb_in = jnp.sum(jnp.transpose(acc_bin[...]), axis=0, keepdims=True)
    gb_col = jnp.sum(acc_bout[...], axis=1, keepdims=True)
    loss_col = jnp.sum(acc_loss[...], axis=1, keepdims=True)
    tail = jnp.sum(
        jnp.where(lane == row, gb_col * (1.0 / units), 0.0) + jnp.where(lane == VP, loss_col, 0.0),
        axis=0, keepdims=True,
    )
    first = small[...] * (1.0 / units)
    first = first + jnp.where(row == V, gb_in, 0.0) + jnp.where(row == V + 1, tail, 0.0)
    small[...] = first
    copy_sa = remote(small, small_a, sa_s, sa_r, (e, partner))
    copy_sa.start()

    half = C // 2
    rows_b = half // E
    scatter_c = rows_b % (16 * Z) == 0
    rows_c = rows_b // Z if scatter_c else rows_b
    theirs = pl.multiple_of((1 - c) * half, half)
    mine = pl.multiple_of(c * half, half)
    gw_send[...] = dot_nt(feat[pl.ds(theirs, half), :], dpre[...]).astype(BF16)
    copy_a = remote(gw_send, recv_a, a_s, a_r, (e, partner))
    copy_a.start()

    copy_sa.wait()
    small[...] = small[...] + small_a[...]
    copies_sb = [remote(small, small_b.at[d - 1], sb_s.at[d - 1], sb_r.at[d - 1], (ens_peer(d), s)) for d in range(1, E)]
    for copy in copies_sb:
        copy.start()

    sum_a[...] = dot_nt(feat[pl.ds(mine, half), :], dpre[...])
    copy_a.wait()
    sum_a[...] = sum_a[...] + recv_a[...].astype(F32)
    send_b[...] = sum_a[...].astype(BF16)
    copies_b = [
        remote(
            send_b.at[pl.ds(pl.multiple_of(ens_peer(d) * rows_b, rows_b), rows_b)],
            recv_b.at[d - 1], b_s.at[d - 1], b_r.at[d - 1], (ens_peer(d), s),
        )
        for d in range(1, E)
    ]
    for copy in copies_b:
        copy.start()

    for copy in copies_sb:
        copy.wait()
    total = small[...]
    for d in range(1, E):
        total = total + small_b[d - 1]
    small[...] = total
    copies_sc = [remote(small, small_c.at[d - 1], sc_s.at[d - 1], sc_r.at[d - 1], (e, 2 * z_peer(d) + c)) for d in range(1, Z)]
    for copy in copies_sc:
        copy.start()

    node_grad[...] = jnp.zeros_like(node_grad)

    def spread_back(i, carry):
        at = lanes(i)
        df = dot(w_in[...], dpre[:, at]).astype(BF16)
        node_grad[...] += dot_nt(table[pl.ds(0, table_len), at], df)
        return carry

    lax.fori_loop(0, tiles, spread_back, 0)
    rim_send[0] = node_grad[pl.ds(R + nodes, R)].astype(BF16)
    rim_send[1] = node_grad[pl.ds(0, R)].astype(BF16)
    rim_up = remote(rim_send.at[0], rim_recv.at[0], rim_s.at[0], rim_r.at[0], (e, s + 1))
    rim_down = remote(rim_send.at[1], rim_recv.at[1], rim_s.at[1], rim_r.at[1], (e, s - 1))

    @pl.when(s < S - 1)
    def _():
        rim_up.start()

    @pl.when(s > 0)
    def _():
        rim_down.start()

    for copy in copies_b:
        copy.wait()
    total = sum_a[pl.ds(pl.multiple_of(e * rows_b, rows_b), rows_b)]
    for d in range(1, E):
        total = total + recv_b[d - 1].astype(F32)
    sum_b[...] = total
    send_c[...] = total.astype(BF16)
    copies_c = []
    for d in range(1, Z):
        if scatter_c:
            src = send_c.at[pl.ds(pl.multiple_of(z_peer(d) * rows_c, rows_c), rows_c)]
        else:
            src = send_c
        copies_c.append(remote(src, recv_c.at[d - 1], c_s.at[d - 1], c_r.at[d - 1], (e, 2 * z_peer(d) + c)))
    for copy in copies_c:
        copy.start()

    node_out[...] = node_grad[pl.ds(R, nodes)]

    @pl.when(s > 0)
    def _():
        rim_up.wait_recv()
        node_out[pl.ds(0, R)] += rim_recv[0].astype(F32)
        rim_down.wait_send()
        down.wait_send()

    @pl.when(s < S - 1)
    def _():
        rim_down.wait_recv()
        node_out[pl.ds(nodes - R, R)] += rim_recv[1].astype(F32)
        rim_up.wait_send()
        up.wait_send()

    def drain(i, carry):
        for d in range(1, E):
            fc_copy(i, d).wait_send()
        return carry

    lax.fori_loop(0, tiles, drain, 0)
    for copy in copies_sc:
        copy.wait()
    total = small[...]
    for d in range(1, Z):
        total = total + small_c[d - 1]
    small_out[...] = total

    base_b = pl.multiple_of(c * half + e * rows_b, rows_b)
    for copy in copies_c:
        copy.wait()
    if scatter_c:
        base_c = pl.multiple_of(base_b + z * rows_c, rows_c)
        total = sum_b[pl.ds(pl.multiple_of(z * rows_c, rows_c), rows_c)]
    else:
        base_c = base_b
        total = sum_b[...]
    for d in range(1, Z):
        total = total + recv_c[d - 1].astype(F32)
    gout[pl.ds(base_c, rows_c)] = total.astype(BF16)
    if scatter_c:
        piece = gout.at[pl.ds(base_c, rows_c)]
        copies_gc = [remote(piece, piece, gc_s.at[d - 1], gc_r.at[d - 1], (e, 2 * z_peer(d) + c)) for d in range(1, Z)]
        for copy in copies_gc:
            copy.start()
        for d in range(1, Z):
            copies_gc[d - 1].wait()
    piece = gout.at[pl.ds(base_b, rows_b)]
    copies_gb = [remote(piece, piece, gb_s.at[d - 1], gb_r.at[d - 1], (ens_peer(d), s)) for d in range(1, E)]
    for copy in copies_gb:
        copy.start()
    copies_ga = []
    for d in range(E):
        if d:
            copies_gb[d - 1].wait_recv()
        at = pl.multiple_of(c * half + lax.rem(e + E - d, E) * rows_b, rows_b)
        piece = gout.at[pl.ds(at, rows_b)]
        copy = remote(piece, piece, ga_s.at[d], ga_r.at[d], (e, partner))
        copy.start()
        copies_ga.append(copy)
    for copy in copies_gb:
        copy.wait_send()
    for copy in copies_ga:
        copy.wait()
    gw_out_ref[...] = gout[...]


def per_device(
    node_latent, point_skip, edge_index, edge_weight, w_in, b_in, readout_matrix, output_bias, truth
):
    members, nodes, C = node_latent.shape
    assert members == 1
    pts = point_skip.shape[0]
    H = w_in.shape[1]
    V = truth.shape[0]
    E = lax.axis_size("ens")
    S = lax.axis_size("space")
    Z = S // 2
    R = nodes // 8
    VP = 16
    T = min(512, pts // 2)
    tiles = pts // T
    table_len = nodes + 2 * R
    half = C // 2
    rows_b = half // E
    rows_c = rows_b // Z if rows_b % (16 * Z) == 0 else rows_b
    vmem = pl.BlockSpec(memory_space=pltpu.VMEM)
    dma = pltpu.SemaphoreType.DMA
    node_grad, gw, small = pl.pallas_call(
        functools.partial(kernel, (E, S, T, R)),
        out_shape=(
            jax.ShapeDtypeStruct((nodes, C), F32),
            jax.ShapeDtypeStruct((C, H), BF16),
            jax.ShapeDtypeStruct((VP, H), F32),
        ),
        in_specs=[vmem, pl.BlockSpec(memory_space=pl.ANY)] + [vmem] * 7,
        out_specs=(vmem, vmem, vmem),
        scratch_shapes=[
            pltpu.VMEM((pts, C), BF16),
            pltpu.VMEM((2 * table_len, C), BF16),
            pltpu.VMEM((C, 2 * table_len), BF16),
            pltpu.VMEM((2 * table_len, pts), BF16),
            pltpu.VMEM((H, C), BF16),
            pltpu.VMEM((C, pts), BF16),
            pltpu.VMEM((H, pts), BF16),
            pltpu.VMEM((H, pts), F32),
            pltpu.VMEM((H, pts), BF16),
            pltpu.VMEM((tiles, V, T), F32),
            pltpu.VMEM((tiles, E - 1, V, T), F32),
            pltpu.VMEM((VP, H), F32),
            pltpu.VMEM((VP, pts), F32),
            pltpu.VMEM((H, 128), F32),
            pltpu.VMEM((H, 128), F32),
            pltpu.VMEM((VP, T), F32),
            pltpu.VMEM((VP, T), F32),
            pltpu.VMEM((table_len, C), F32),
            pltpu.VMEM((2, R, C), BF16),
            pltpu.VMEM((2, R, C), BF16),
            pltpu.VMEM((half, H), BF16),
            pltpu.VMEM((half, H), F32),
            pltpu.VMEM((half, H), BF16),
            pltpu.VMEM((half, H), BF16),
            pltpu.VMEM((rows_b, H), F32),
            pltpu.VMEM((E - 1, rows_b, H), BF16),
            pltpu.VMEM((rows_b, H), BF16),
            pltpu.VMEM((Z - 1, rows_c, H), BF16),
            pltpu.VMEM((C, H), BF16),
            pltpu.VMEM((VP, H), F32),
            pltpu.VMEM((VP, H), F32),
            pltpu.VMEM((E - 1, VP, H), F32),
            pltpu.VMEM((Z - 1, VP, H), F32),
            dma, dma((2,)), dma((2,)),
            dma((tiles, E - 1)), dma((tiles, E - 1)),
            dma((2,)), dma((2,)),
            dma, dma,
            dma((E - 1,)), dma((E - 1,)),
            dma((Z - 1,)), dma((Z - 1,)),
            dma((Z - 1,)), dma((Z - 1,)),
            dma((E - 1,)), dma((E - 1,)),
            dma((E,)), dma((E,)),
            dma, dma,
            dma((E - 1,)), dma((E - 1,)),
            dma((Z - 1,)), dma((Z - 1,)),
        ],
        compiler_params=pltpu.CompilerParams(
            collective_id=0, has_side_effects=True, vmem_limit_bytes=52 * 2**20
        ),
        cost_estimate=pl.CostEstimate(flops=8 * 10**9, bytes_accessed=5 * 10**6, transcendentals=2 * 10**6),
    )(
        node_latent[0], point_skip, edge_index, edge_weight, w_in, b_in[None], readout_matrix,
        jnp.pad(output_bias, (0, 128 - V))[None], truth,
    )
    points = pts * S
    scale = 1.0 / math.sqrt(E * points)
    loss = small[V + 1, VP] / (points * V)
    return (
        loss, node_grad[None], gw.astype(F32) * scale, small[V] * scale,
        small[:V] * scale, small[V + 1, :V] * scale,
    )


def solution(mesh):
    return jax.shard_map(
        per_device,
        mesh=mesh,
        in_specs=(
            P("ens", "space", None), P("space", None), P(None, "space"), P(None, "space"),
            P(), P(), P(), P(), P(None, "space"),
        ),
        out_specs=(P(), P("ens", "space", None), P(), P(), P(), P()),
        check_vma=False,
    )
```

```python
import functools
import math

import jax
import jax.numpy as jnp
from jax import lax
from jax.experimental import pallas as pl
from jax.experimental.pallas import tpu as pltpu
from jax.sharding import PartitionSpec as P

UNBIASING = 0.95
F32 = jnp.float32
BF16 = jnp.bfloat16
NT = (((1,), (1,)), ((), ()))


def dot(a, b):
    return jnp.dot(a, b, preferred_element_type=F32)


def dot_nt(a, b):
    return lax.dot_general(a, b, NT, preferred_element_type=F32)


def sign(x):
    return jnp.where(x > 0, 1.0, 0.0) - jnp.where(x < 0, 1.0, 0.0)


def kernel(
    cfg,
    latent_hbm, skip_hbm, index_hbm, weight_hbm, w_in_hbm, b_in_hbm, readout_hbm, bias_hbm, truth_hbm,
    node_hbm, gw_hbm, small_hbm,
    latent, skip, index, weight, w_in, b_in, readout, bias, truth, ext, ext_t, table, w_t, feat, hid, slope, dpre, fc, fc_in,
    ro_pad, truth_pad, b_col, acc_bin, acc_bout, acc_loss, node_grad,
    rim_send, rim_recv, gw, gw_send, sum_a, recv_a, send_b, sum_b, recv_b, send_c, recv_c, gout,
    small, small_send, small_a, small_b, small_c,
    local_sem, out_sem, halo_s, halo_r, fc_s, fc_r, rim_s, rim_r, a_s, a_r, b_s, b_r, c_s, c_r,
    gc_s, gc_r, gb_s, gb_r, ga_s, ga_r, sa_s, sa_r, sb_s, sb_r, sc_s, sc_r,
):
    E, S, T, R, Q = cfg
    Z = S // 2
    nodes, C = latent.shape
    H = w_in.shape[1]
    pts = skip.shape[0]
    K = index.shape[0]
    V = readout.shape[0]
    VP = ro_pad.shape[0]
    tiles = pts // T
    table_len = nodes + 2 * R
    e = lax.axis_index("ens")
    s = lax.axis_index("space")
    c = lax.rem(s, 2)
    z = lax.div(s, 2)
    partner = s + 1 - 2 * c
    far = s - 1 + 2 * c
    has_far = jnp.logical_and(far >= 0, far < S)

    loads = [
        pltpu.make_async_copy(src, dst, local_sem.at[i])
        for i, (src, dst) in enumerate((
            (index_hbm, index), (weight_hbm, weight), (latent_hbm, latent), (w_in_hbm, w_in), (b_in_hbm, b_in),
            (readout_hbm, readout), (bias_hbm, bias), (truth_hbm, truth), (skip_hbm, skip),
        ))
    ]
    for load in loads:
        load.start()

    barrier = pltpu.get_barrier_semaphore()

    def greet(dev):
        pl.semaphore_signal(barrier, inc=1, device_id=dev, device_id_type=pl.DeviceIdType.MESH)

    def ens_peer(d):
        return lax.rem(e + d, E)

    def z_peer(d):
        return lax.rem(z + d, Z)

    greet((e, partner))
    for d in range(1, E):
        greet((ens_peer(d), s))
    for d in range(1, Z):
        greet((e, 2 * z_peer(d) + c))

    @pl.when(has_far)
    def _():
        greet((e, far))

    def remote(src, dst, ss, rs, dev):
        return pltpu.make_async_remote_copy(
            src_ref=src, dst_ref=dst, send_sem=ss, recv_sem=rs,
            device_id=dev, device_id_type=pl.DeviceIdType.MESH,
        )

    for load in loads[:-1]:
        load.wait()
    ext[pl.ds(R, nodes)] = latent[...]
    ext[pl.ds(table_len + R, nodes)] = latent[...]
    w_t[...] = jnp.transpose(w_in[...])
    b_col[...] = jnp.transpose(jnp.broadcast_to(b_in[...], (128, H)))
    ro_pad[...] = jnp.zeros_like(ro_pad)
    ro_pad[pl.ds(0, V)] = readout[...].astype(F32)
    truth_pad[...] = jnp.zeros_like(truth_pad)
    truth_pad[pl.ds(0, V)] = truth[...]
    acc_bin[...] = jnp.zeros_like(acc_bin)
    acc_bout[...] = jnp.zeros_like(acc_bout)
    acc_loss[...] = jnp.zeros_like(acc_loss)
    small[...] = jnp.zeros_like(small)
    ro = ro_pad[...].astype(BF16)
    ro_t = jnp.transpose(ro_pad[...]).astype(BF16)
    row_v = lax.broadcasted_iota(jnp.int32, (VP, V), 0)
    lane_v = lax.broadcasted_iota(jnp.int32, (VP, V), 1)
    bias_col = jnp.sum(
        jnp.where(row_v == lane_v, jnp.broadcast_to(bias[...], (VP, V)), 0.0), axis=1, keepdims=True
    )

    def lanes(i):
        return pl.ds(pl.multiple_of(i * T, T), T)

    def make_table(i, carry):
        slot = lax.broadcasted_iota(jnp.int32, (table_len, T), 0)
        total = jnp.zeros((table_len, T), F32)
        for k in range(K):
            total = total + jnp.where(slot == index[pl.ds(k, 1), lanes(i)], weight[pl.ds(k, 1), lanes(i)], 0.0)
        high = total.astype(BF16)
        table[pl.ds(0, table_len), lanes(i)] = high
        table[pl.ds(table_len, table_len), lanes(i)] = (total - high.astype(F32)).astype(BF16)
        return carry

    lax.fori_loop(0, tiles // 2, make_table, 0)

    pl.semaphore_wait(barrier, E + Z - 1 + has_far.astype(jnp.int32))

    up = remote(latent.at[pl.ds(nodes - R, R)], ext.at[pl.ds(0, R)], halo_s.at[0], halo_r.at[0], (e, s + 1))
    down = remote(latent.at[pl.ds(0, R)], ext.at[pl.ds(R + nodes, R)], halo_s.at[1], halo_r.at[1], (e, s - 1))

    @pl.when(s < S - 1)
    def _():
        up.start()

    @pl.when(s > 0)
    def _():
        down.start()

    @pl.when(s == 0)
    def _():
        ext[pl.ds(0, R)] = jnp.zeros((R, C), BF16)

    @pl.when(s == S - 1)
    def _():
        ext[pl.ds(R + nodes, R)] = jnp.zeros((R, C), BF16)

    lax.fori_loop(tiles // 2, tiles, make_table, 0)
    loads[-1].wait()

    @pl.when(s < S - 1)
    def _():
        down.wait_recv()

    @pl.when(s > 0)
    def _():
        up.wait_recv()

    ext[pl.ds(table_len, R)] = ext[pl.ds(0, R)]
    ext[pl.ds(table_len + R + nodes, R)] = ext[pl.ds(R + nodes, R)]
    ext_t[...] = jnp.transpose(ext[...])

    units = 20.0 * E * (E - 1)
    from_truth = 20.0 * (E - 1)
    from_pair = 20.0 * UNBIASING

    def fc_copy(i, d):
        return remote(fc.at[i], fc_in.at[i, d - 1], fc_s.at[i, d - 1], fc_r.at[i, d - 1], (ens_peer(d), s))

    def forward(i, carry):
        at = lanes(i)
        skip_t = jnp.transpose(skip[at, :]).astype(F32)
        f = (skip_t + dot(ext_t[...], table[:, at])).astype(BF16)
        feat[:, at] = f
        col = b_col[...]
        pre = dot(w_t[...], f) + jnp.concatenate([col] * (T // 128), axis=1)
        sig = 1.0 / (1.0 + jnp.exp(-pre))
        h = pre * sig
        slope[:, at] = (sig + h * (1.0 - sig)) * (1.0 / units)
        hb = h.astype(BF16)
        hid[:, at] = hb
        fc[i] = (dot(ro, hb) + bias_col)[:V]
        for d in range(1, E):
            fc_copy(i, d).start()
        return carry

    lax.fori_loop(0, tiles, forward, 0)

    def backward(i, carry):
        at = lanes(i)
        for d in range(1, E):
            fc_copy(i, d).wait_recv()
        own = fc[i]
        gap = own - truth_pad[pl.ds(0, V), at]
        pairs = jnp.zeros_like(own)
        spread = jnp.zeros_like(own)
        for d in range(1, E):
            diff = own - fc_in[i, d - 1]
            pairs = pairs + sign(diff)
            spread = spread + jnp.abs(diff)
        adj = from_truth * sign(gap) - from_pair * pairs
        acc_bout[pl.ds(0, V)] += adj
        acc_loss[pl.ds(0, V)] += jnp.abs(gap) * (1.0 / E) - spread * (UNBIASING / (2.0 * E * (E - 1)))
        truth_pad[pl.ds(0, V), at] = adj
        g = truth_pad[:, at].astype(BF16)
        small[...] += dot_nt(g, hid[:, at])
        dp = (dot(ro_t, g) * slope[:, at]).astype(BF16)
        dpre[:, at] = dp
        dp32 = dp.astype(F32)
        part = dp32[:, 0:128]
        for j in range(1, T // 128):
            part = part + dp32[:, j * 128:(j + 1) * 128]
        acc_bin[...] += part
        return carry

    lax.fori_loop(0, tiles - 1, backward, 0)
    done = (tiles - 1) * T
    gw[...] = dot_nt(feat[:, :done], dpre[:, :done])
    lax.fori_loop(tiles - 1, tiles, backward, 0)

    row = lax.broadcasted_iota(jnp.int32, (VP, H), 0)
    lane = lax.broadcasted_iota(jnp.int32, (VP, H), 1)
    gb_in = jnp.sum(jnp.transpose(acc_bin[...]), axis=0, keepdims=True)
    gb_col = jnp.sum(acc_bout[...], axis=1, keepdims=True)
    loss_col = jnp.sum(acc_loss[...], axis=1, keepdims=True)
    tail = jnp.sum(
        jnp.where(lane == row, gb_col * (1.0 / units), 0.0) + jnp.where(lane == VP, loss_col, 0.0),
        axis=0, keepdims=True,
    )
    first = small[...] * (1.0 / units)
    first = first + jnp.where(row == V, gb_in, 0.0) + jnp.where(row == V + 1, tail, 0.0)
    small[...] = first

    def pack_small():
        value = small[...]
        high = value.astype(BF16).astype(F32)
        low = jnp.broadcast_to((value - high)[V + 1:V + 2], (VP, H))
        small_send[...] = jnp.where(row == V + 2, low, high).astype(BF16)

    def add_small(*terms):
        total = small[...]
        for term in terms:
            total = total + term.astype(F32)
        low = jnp.broadcast_to(total[V + 2:V + 3], (VP, H))
        small[...] = jnp.where(row == V + 1, total + low, jnp.where(row == V + 2, 0.0, total))

    pack_small()
    copy_sa = remote(small_send, small_a, sa_s, sa_r, (e, partner))
    copy_sa.start()

    half = C // 2
    cols = H // Q
    rows_b = half // E
    scatter_c = rows_b % (16 * Z) == 0
    rows_c = rows_b // Z if scatter_c else rows_b
    theirs = pl.multiple_of((1 - c) * half, half)
    mine = pl.multiple_of(c * half, half)

    def last_part(rows, q):
        at = pl.ds(q * cols, cols)
        return gw[pl.ds(rows, half), at] + dot_nt(feat[pl.ds(rows, half), done:], dpre[at, done:])

    copies_a = []
    for q in range(Q):
        gw_send[q] = last_part(theirs, q).astype(BF16)
        copy = remote(gw_send.at[q], recv_a.at[q], a_s.at[q], a_r.at[q], (e, partner))
        copy.start()
        copies_a.append(copy)

    copy_sa.wait()
    add_small(small_a[...])
    pack_small()
    copies_sb = [remote(small_send, small_b.at[d - 1], sb_s.at[d - 1], sb_r.at[d - 1], (ens_peer(d), s)) for d in range(1, E)]
    for copy in copies_sb:
        copy.start()

    copies_b = []
    for q in range(Q):
        own = last_part(mine, q)
        copies_a[q].wait()
        own = own + recv_a[q].astype(F32)
        sum_a[q] = own
        send_b[q] = own.astype(BF16)
        parts = [
            remote(
                send_b.at[q, pl.ds(pl.multiple_of(ens_peer(d) * rows_b, rows_b), rows_b)],
                recv_b.at[q, d - 1], b_s.at[q, d - 1], b_r.at[q, d - 1], (ens_peer(d), s),
            )
            for d in range(1, E)
        ]
        for copy in parts:
            copy.start()
        copies_b.append(parts)

    node_grad[...] = jnp.zeros_like(node_grad)
    wide = pts // 2

    def spread_back(i):
        at = pl.ds(i * wide, wide)
        df = dot(w_in[...], dpre[:, at]).astype(BF16)
        node_grad[...] += dot_nt(table[pl.ds(0, table_len), at], df)

    spread_back(0)
    for copy in copies_sb:
        copy.wait()
    add_small(*[small_b[d - 1] for d in range(1, E)])
    pack_small()
    copies_sc = [remote(small_send, small_c.at[d - 1], sc_s.at[d - 1], sc_r.at[d - 1], (e, 2 * z_peer(d) + c)) for d in range(1, Z)]
    for copy in copies_sc:
        copy.start()

    def stage_c(q):
        for copy in copies_b[q]:
            copy.wait()
        total = sum_a[q, pl.ds(pl.multiple_of(e * rows_b, rows_b), rows_b)]
        for d in range(1, E):
            total = total + recv_b[q, d - 1].astype(F32)
        sum_b[q] = total
        send_c[q] = total.astype(BF16)
        parts = []
        for d in range(1, Z):
            if scatter_c:
                src = send_c.at[q, pl.ds(pl.multiple_of(z_peer(d) * rows_c, rows_c), rows_c)]
            else:
                src = send_c.at[q]
            parts.append(remote(src, recv_c.at[q, d - 1], c_s.at[q, d - 1], c_r.at[q, d - 1], (e, 2 * z_peer(d) + c)))
        for copy in parts:
            copy.start()
        return parts

    copies_c = [stage_c(0)]
    spread_back(1)
    for q in range(1, Q):
        copies_c.append(stage_c(q))

    rim_send[0] = node_grad[pl.ds(R + nodes, R)].astype(BF16)
    rim_send[1] = node_grad[pl.ds(0, R)].astype(BF16)
    rim_up = remote(rim_send.at[0], rim_recv.at[0], rim_s.at[0], rim_r.at[0], (e, s + 1))
    rim_down = remote(rim_send.at[1], rim_recv.at[1], rim_s.at[1], rim_r.at[1], (e, s - 1))

    @pl.when(s < S - 1)
    def _():
        rim_up.start()

    @pl.when(s > 0)
    def _():
        rim_down.start()

    base_b = pl.multiple_of(c * half + e * rows_b, rows_b)
    base_c = pl.multiple_of(base_b + z * rows_c, rows_c) if scatter_c else base_b
    copies_gc = []
    for q in range(Q):
        for copy in copies_c[q]:
            copy.wait()
        if scatter_c:
            total = sum_b[q, pl.ds(pl.multiple_of(z * rows_c, rows_c), rows_c)]
        else:
            total = sum_b[q]
        for d in range(1, Z):
            total = total + recv_c[q, d - 1].astype(F32)
        gout[q, pl.ds(base_c, rows_c)] = total.astype(BF16)
        parts = []
        if scatter_c:
            piece = gout.at[q, pl.ds(base_c, rows_c)]
            parts = [remote(piece, piece, gc_s.at[q, d - 1], gc_r.at[q, d - 1], (e, 2 * z_peer(d) + c)) for d in range(1, Z)]
            for copy in parts:
                copy.start()
        copies_gc.append(parts)

    def to_partner(q, d):
        at = pl.multiple_of(c * half + lax.rem(e + E - d, E) * rows_b, rows_b)
        piece = gout.at[q, pl.ds(at, rows_b)]
        return remote(piece, piece, ga_s.at[q, d], ga_r.at[q, d], (e, partner))

    copies_gb = []
    for q in range(Q):
        for copy in copies_gc[q]:
            copy.wait()
        piece = gout.at[q, pl.ds(base_b, rows_b)]
        parts = [remote(piece, piece, gb_s.at[q, d - 1], gb_r.at[q, d - 1], (ens_peer(d), s)) for d in range(1, E)]
        for copy in parts:
            copy.start()
        to_partner(q, 0).start()
        copies_gb.append(parts)

    @pl.when(s > 0)
    def _():
        rim_up.wait_recv()
        node_grad[pl.ds(R, R)] += rim_recv[0].astype(F32)
        rim_down.wait_send()
        down.wait_send()

    @pl.when(s < S - 1)
    def _():
        rim_down.wait_recv()
        node_grad[pl.ds(nodes, R)] += rim_recv[1].astype(F32)
        rim_up.wait_send()
        up.wait_send()

    stores = [pltpu.make_async_copy(node_grad.at[pl.ds(R, nodes)], node_hbm, out_sem.at[0])]
    stores[0].start()
    for copy in copies_sc:
        copy.wait()
    add_small(*[small_c[d - 1] for d in range(1, Z)])
    stores.append(pltpu.make_async_copy(small, small_hbm, out_sem.at[1]))
    stores[1].start()

    def drain(i, carry):
        for d in range(1, E):
            fc_copy(i, d).wait_send()
        return carry

    lax.fori_loop(0, tiles, drain, 0)
    for q in range(Q):
        for d in range(1, E):
            copies_gb[q][d - 1].wait_recv()
            to_partner(q, d).start()
    for q in range(Q):
        for copy in copies_gb[q]:
            copy.wait_send()
        for d in range(E):
            to_partner(q, d).wait()
    stores.append(pltpu.make_async_copy(gout, gw_hbm, out_sem.at[2]))
    stores[2].start()
    for store in stores:
        store.wait()


def finish(
    scale, loss_scale, V, lane,
    node_in, gw_in, small_in, loss_hbm, node_hbm, gw_hbm, b_in_hbm, w_out_hbm, b_out_hbm,
    gw, small, loss, gw_f, b_in, w_out, b_out, sems,
):
    Q, _, cols = gw.shape
    loads = [pltpu.make_async_copy(gw_in.at[q], gw.at[q], sems.at[7 + q]) for q in range(Q)]
    loads.append(pltpu.make_async_copy(small_in, small, sems.at[7 + Q]))
    for load in loads:
        load.start()
    copies = [pltpu.make_async_copy(node_in, node_hbm, sems.at[0])]
    copies[0].start()
    for q in range(Q):
        loads[q].wait()
        at = pl.ds(q * cols, cols)
        gw_f[:, at] = gw[q].astype(F32) * scale
        copies.append(pltpu.make_async_copy(gw_f.at[:, at], gw_hbm.at[:, at], sems.at[1 + q]))
        copies[-1].start()
    loads[Q].wait()
    loss[...] = small[V + 1:V + 2, lane:lane + 1] * loss_scale
    b_in[...] = small[V:V + 1, :] * scale
    w_out[...] = small[:V, :] * scale
    b_out[...] = small[V + 1:V + 2, :V] * scale
    for i, (src, dst) in enumerate(((loss, loss_hbm), (b_in, b_in_hbm), (w_out, w_out_hbm), (b_out, b_out_hbm))):
        copies.append(pltpu.make_async_copy(src, dst, sems.at[3 + i]))
        copies[-1].start()
    for copy in copies:
        copy.wait()


def per_device(
    node_latent, point_skip, edge_index, edge_weight, w_in, b_in, readout_matrix, output_bias, truth
):
    members, nodes, C = node_latent.shape
    assert members == 1
    pts = point_skip.shape[0]
    H = w_in.shape[1]
    V = truth.shape[0]
    E = lax.axis_size("ens")
    S = lax.axis_size("space")
    Z = S // 2
    R = nodes // 8
    VP = 16
    Q = 2
    cols = H // Q
    K = edge_index.shape[0]
    T = min(512, pts // 2)
    tiles = pts // T
    table_len = nodes + 2 * R
    half = C // 2
    rows_b = half // E
    rows_c = rows_b // Z if rows_b % (16 * Z) == 0 else rows_b
    hbm = pl.BlockSpec(memory_space=pltpu.HBM)
    dma = pltpu.SemaphoreType.DMA
    node_grad, gw, small = pl.pallas_call(
        functools.partial(kernel, (E, S, T, R, Q)),
        out_shape=(
            jax.ShapeDtypeStruct((nodes, C), F32),
            jax.ShapeDtypeStruct((Q, C, cols), BF16),
            jax.ShapeDtypeStruct((VP, H), F32),
        ),
        in_specs=[hbm] * 9,
        out_specs=(hbm, hbm, hbm),
        scratch_shapes=[
            pltpu.VMEM((nodes, C), BF16),
            pltpu.VMEM((pts, C), BF16),
            pltpu.VMEM((K, pts), jnp.int32),
            pltpu.VMEM((K, pts), F32),
            pltpu.VMEM((C, H), BF16),
            pltpu.VMEM((1, H), F32),
            pltpu.VMEM((V, H), BF16),
            pltpu.VMEM((1, V), F32),
            pltpu.VMEM((V, pts), F32),
            pltpu.VMEM((2 * table_len, C), BF16),
            pltpu.VMEM((C, 2 * table_len), BF16),
            pltpu.VMEM((2 * table_len, pts), BF16),
            pltpu.VMEM((H, C), BF16),
            pltpu.VMEM((C, pts), BF16),
            pltpu.VMEM((H, pts), BF16),
            pltpu.VMEM((H, pts), F32),
            pltpu.VMEM((H, pts), BF16),
            pltpu.VMEM((tiles, V, T), F32),
            pltpu.VMEM((tiles, E - 1, V, T), F32),
            pltpu.VMEM((VP, H), F32),
            pltpu.VMEM((VP, pts), F32),
            pltpu.VMEM((H, 128), F32),
            pltpu.VMEM((H, 128), F32),
            pltpu.VMEM((VP, T), F32),
            pltpu.VMEM((VP, T), F32),
            pltpu.VMEM((table_len, C), F32),
            pltpu.VMEM((2, R, C), BF16),
            pltpu.VMEM((2, R, C), BF16),
            pltpu.VMEM((C, H), F32),
            pltpu.VMEM((Q, half, cols), BF16),
            pltpu.VMEM((Q, half, cols), F32),
            pltpu.VMEM((Q, half, cols), BF16),
            pltpu.VMEM((Q, half, cols), BF16),
            pltpu.VMEM((Q, rows_b, cols), F32),
            pltpu.VMEM((Q, E - 1, rows_b, cols), BF16),
            pltpu.VMEM((Q, rows_b, cols), BF16),
            pltpu.VMEM((Q, Z - 1, rows_c, cols), BF16),
            pltpu.VMEM((Q, C, cols), BF16),
            pltpu.VMEM((VP, H), F32),
            pltpu.VMEM((VP, H), BF16),
            pltpu.VMEM((VP, H), BF16),
            pltpu.VMEM((E - 1, VP, H), BF16),
            pltpu.VMEM((Z - 1, VP, H), BF16),
            dma((9,)), dma((3,)), dma((2,)), dma((2,)),
            dma((tiles, E - 1)), dma((tiles, E - 1)),
            dma((2,)), dma((2,)),
            dma((Q,)), dma((Q,)),
            dma((Q, E - 1)), dma((Q, E - 1)),
            dma((Q, Z - 1)), dma((Q, Z - 1)),
            dma((Q, Z - 1)), dma((Q, Z - 1)),
            dma((Q, E - 1)), dma((Q, E - 1)),
            dma((Q, E)), dma((Q, E)),
            dma, dma,
            dma((E - 1,)), dma((E - 1,)),
            dma((Z - 1,)), dma((Z - 1,)),
        ],
        compiler_params=pltpu.CompilerParams(
            collective_id=0, has_side_effects=True, vmem_limit_bytes=62 * 2**20
        ),
        cost_estimate=pl.CostEstimate(flops=8 * 10**9, bytes_accessed=5 * 10**6, transcendentals=2 * 10**6),
    )(
        node_latent[0], point_skip, edge_index, edge_weight, w_in, b_in[None], readout_matrix,
        output_bias[None], truth,
    )
    points = pts * S
    scale = 1.0 / math.sqrt(E * points)
    sds = jax.ShapeDtypeStruct
    loss, node_grad, gw, gb_in, gw_out, gb_out = pl.pallas_call(
        functools.partial(finish, scale, 1.0 / (points * V), V, VP),
        out_shape=(
            sds((1, 1), F32), sds((nodes, C), F32), sds((C, H), F32),
            sds((1, H), F32), sds((V, H), F32), sds((1, V), F32),
        ),
        in_specs=[hbm] * 3,
        out_specs=(hbm,) * 6,
        scratch_shapes=[
            pltpu.VMEM((Q, C, cols), BF16), pltpu.VMEM((VP, H), F32),
            pltpu.VMEM((1, 1), F32), pltpu.VMEM((C, H), F32), pltpu.VMEM((1, H), F32),
            pltpu.VMEM((V, H), F32), pltpu.VMEM((1, V), F32), dma((8 + Q,)),
        ],
        compiler_params=pltpu.CompilerParams(vmem_limit_bytes=62 * 2**20),
    )(node_grad, gw, small)
    return loss[0, 0], node_grad[None], gw, gb_in[0], gw_out, gb_out[0]


def solution(mesh):
    return jax.shard_map(
        per_device,
        mesh=mesh,
        in_specs=(
            P("ens", "space", None), P("space", None), P(None, "space"), P(None, "space"),
            P(), P(), P(), P(), P(None, "space"),
        ),
        out_specs=(P(), P("ens", "space", None), P(), P(), P(), P()),
        check_vma=False,
    )
```

```python
import functools
import math

import jax
import jax.numpy as jnp
from jax import lax
from jax.experimental import pallas as pl
from jax.experimental.pallas import tpu as pltpu
from jax.sharding import PartitionSpec as P

UNBIASING = 0.95
F32 = jnp.float32
BF16 = jnp.bfloat16
NT = (((1,), (1,)), ((), ()))


def dot(a, b):
    return jnp.dot(a, b, preferred_element_type=F32)


def dot_nt(a, b):
    return lax.dot_general(a, b, NT, preferred_element_type=F32)


def sign(x):
    return jnp.where(x > 0, 1.0, 0.0) - jnp.where(x < 0, 1.0, 0.0)


def kernel(
    cfg,
    latent_hbm, skip_hbm, index_hbm, weight_hbm, w_in_hbm, b_in_hbm, readout_hbm, bias_hbm, truth_hbm,
    node_hbm, gw_hbm, small_hbm,
    latent, skip, index, weight, w_in, b_in, readout, bias, truth, ext, ext_t, table, w_t, feat, hid, slope, dpre, fc, fc_in,
    ro_pad, truth_pad, b_col, acc_bin, acc_bout, acc_loss, node_grad,
    rim_send, rim_recv, gw, gw_send, sum_a, recv_a, send_b, sum_b, recv_b, send_c, recv_c, gout,
    small, small_send, small_a, small_b, small_c,
    local_sem, out_sem, halo_s, halo_r, fc_s, fc_r, rim_s, rim_r, a_s, a_r, b_s, b_r, c_s, c_r,
    gc_s, gc_r, gb_s, gb_r, ga_s, ga_r, sa_s, sa_r, sb_s, sb_r, sc_s, sc_r,
):
    E, S, T, R, Q = cfg
    Z = S // 2
    nodes, C = latent.shape
    H = w_in.shape[1]
    pts = skip.shape[0]
    K = index.shape[0]
    V = readout.shape[0]
    VP = ro_pad.shape[0]
    tiles = pts // T
    table_len = nodes + 2 * R
    e = lax.axis_index("ens")
    s = lax.axis_index("space")
    c = lax.rem(s, 2)
    z = lax.div(s, 2)
    partner = s + 1 - 2 * c
    far = s - 1 + 2 * c
    has_far = jnp.logical_and(far >= 0, far < S)

    loads = [
        pltpu.make_async_copy(src, dst, local_sem.at[i])
        for i, (src, dst) in enumerate((
            (index_hbm, index), (weight_hbm, weight), (latent_hbm, latent), (w_in_hbm, w_in), (b_in_hbm, b_in),
            (readout_hbm, readout), (bias_hbm, bias), (truth_hbm, truth), (skip_hbm, skip),
        ))
    ]
    for load in loads:
        load.start()

    barrier = pltpu.get_barrier_semaphore()

    def greet(dev):
        pl.semaphore_signal(barrier, inc=1, device_id=dev, device_id_type=pl.DeviceIdType.MESH)

    def ens_peer(d):
        return lax.rem(e + d, E)

    def z_peer(d):
        return lax.rem(z + d, Z)

    greet((e, partner))
    for d in range(1, E):
        greet((ens_peer(d), s))
    for d in range(1, Z):
        greet((e, 2 * z_peer(d) + c))

    @pl.when(has_far)
    def _():
        greet((e, far))

    def remote(src, dst, ss, rs, dev):
        return pltpu.make_async_remote_copy(
            src_ref=src, dst_ref=dst, send_sem=ss, recv_sem=rs,
            device_id=dev, device_id_type=pl.DeviceIdType.MESH,
        )

    for load in loads[:-1]:
        load.wait()
    ext[pl.ds(R, nodes)] = latent[...]
    ext[pl.ds(table_len + R, nodes)] = latent[...]
    w_t[...] = jnp.transpose(w_in[...])
    b_col[...] = jnp.transpose(jnp.broadcast_to(b_in[...], (128, H)))
    ro_pad[...] = jnp.zeros_like(ro_pad)
    ro_pad[pl.ds(0, V)] = readout[...].astype(F32)
    truth_pad[...] = jnp.zeros_like(truth_pad)
    truth_pad[pl.ds(0, V)] = truth[...]
    acc_bin[...] = jnp.zeros_like(acc_bin)
    acc_bout[...] = jnp.zeros_like(acc_bout)
    acc_loss[...] = jnp.zeros_like(acc_loss)
    small[...] = jnp.zeros_like(small)
    ro = ro_pad[...].astype(BF16)
    ro_t = jnp.transpose(ro_pad[...]).astype(BF16)
    row_v = lax.broadcasted_iota(jnp.int32, (VP, V), 0)
    lane_v = lax.broadcasted_iota(jnp.int32, (VP, V), 1)
    bias_col = jnp.sum(
        jnp.where(row_v == lane_v, jnp.broadcast_to(bias[...], (VP, V)), 0.0), axis=1, keepdims=True
    )

    def lanes(i):
        return pl.ds(pl.multiple_of(i * T, T), T)

    def make_table(i, carry):
        slot = lax.broadcasted_iota(jnp.int32, (table_len, T), 0)
        total = jnp.zeros((table_len, T), F32)
        for k in range(K):
            total = total + jnp.where(slot == index[pl.ds(k, 1), lanes(i)], weight[pl.ds(k, 1), lanes(i)], 0.0)
        high = total.astype(BF16)
        table[pl.ds(0, table_len), lanes(i)] = high
        table[pl.ds(table_len, table_len), lanes(i)] = (total - high.astype(F32)).astype(BF16)
        return carry

    lax.fori_loop(0, tiles // 2, make_table, 0)

    pl.semaphore_wait(barrier, E + Z - 1 + has_far.astype(jnp.int32))

    up = remote(latent.at[pl.ds(nodes - R, R)], ext.at[pl.ds(0, R)], halo_s.at[0], halo_r.at[0], (e, s + 1))
    down = remote(latent.at[pl.ds(0, R)], ext.at[pl.ds(R + nodes, R)], halo_s.at[1], halo_r.at[1], (e, s - 1))

    @pl.when(s < S - 1)
    def _():
        up.start()

    @pl.when(s > 0)
    def _():
        down.start()

    @pl.when(s == 0)
    def _():
        ext[pl.ds(0, R)] = jnp.zeros((R, C), BF16)

    @pl.when(s == S - 1)
    def _():
        ext[pl.ds(R + nodes, R)] = jnp.zeros((R, C), BF16)

    lax.fori_loop(tiles // 2, tiles, make_table, 0)
    loads[-1].wait()

    @pl.when(s < S - 1)
    def _():
        down.wait_recv()

    @pl.when(s > 0)
    def _():
        up.wait_recv()

    ext[pl.ds(table_len, R)] = ext[pl.ds(0, R)]
    ext[pl.ds(table_len + R + nodes, R)] = ext[pl.ds(R + nodes, R)]
    ext_t[...] = jnp.transpose(ext[...])

    units = 20.0 * E * (E - 1)
    from_truth = 20.0 * (E - 1)
    from_pair = 20.0 * UNBIASING

    def fc_copy(i, d):
        return remote(fc.at[i], fc_in.at[i, d - 1], fc_s.at[i, d - 1], fc_r.at[i, d - 1], (ens_peer(d), s))

    def forward(i, carry):
        at = lanes(i)
        skip_t = jnp.transpose(skip[at, :]).astype(F32)
        f = (skip_t + dot(ext_t[...], table[:, at])).astype(BF16)
        feat[:, at] = f
        col = b_col[...]
        pre = dot(w_t[...], f) + jnp.concatenate([col] * (T // 128), axis=1)
        sig = 1.0 / (1.0 + jnp.exp(-pre))
        h = pre * sig
        slope[:, at] = (sig + h * (1.0 - sig)) * (1.0 / units)
        hb = h.astype(BF16)
        hid[:, at] = hb
        fc[i] = (dot(ro, hb) + bias_col)[:V]
        for d in range(1, E):
            fc_copy(i, d).start()
        return carry

    lax.fori_loop(0, tiles, forward, 0)

    def backward(i, carry):
        at = lanes(i)
        for d in range(1, E):
            fc_copy(i, d).wait_recv()
        own = fc[i]
        gap = own - truth_pad[pl.ds(0, V), at]
        pairs = jnp.zeros_like(own)
        spread = jnp.zeros_like(own)
        for d in range(1, E):
            diff = own - fc_in[i, d - 1]
            pairs = pairs + sign(diff)
            spread = spread + jnp.abs(diff)
        adj = from_truth * sign(gap) - from_pair * pairs
        acc_bout[pl.ds(0, V)] += adj
        acc_loss[pl.ds(0, V)] += jnp.abs(gap) * (1.0 / E) - spread * (UNBIASING / (2.0 * E * (E - 1)))
        truth_pad[pl.ds(0, V), at] = adj
        g = truth_pad[:, at].astype(BF16)
        small[...] += dot_nt(g, hid[:, at])
        dp = (dot(ro_t, g) * slope[:, at]).astype(BF16)
        dpre[:, at] = dp
        dp32 = dp.astype(F32)
        part = dp32[:, 0:128]
        for j in range(1, T // 128):
            part = part + dp32[:, j * 128:(j + 1) * 128]
        acc_bin[...] += part
        return carry

    lax.fori_loop(0, tiles - 1, backward, 0)
    done = (tiles - 1) * T
    gw[...] = dot_nt(feat[:, :done], dpre[:, :done])
    lax.fori_loop(tiles - 1, tiles, backward, 0)

    row = lax.broadcasted_iota(jnp.int32, (VP, H), 0)
    lane = lax.broadcasted_iota(jnp.int32, (VP, H), 1)
    gb_in = jnp.sum(jnp.transpose(acc_bin[...]), axis=0, keepdims=True)
    gb_col = jnp.sum(acc_bout[...], axis=1, keepdims=True)
    loss_col = jnp.sum(acc_loss[...], axis=1, keepdims=True)
    tail = jnp.sum(
        jnp.where(lane == row, gb_col * (1.0 / units), 0.0) + jnp.where(lane == VP, loss_col, 0.0),
        axis=0, keepdims=True,
    )
    first = small[...] * (1.0 / units)
    first = first + jnp.where(row == V, gb_in, 0.0) + jnp.where(row == V + 1, tail, 0.0)
    small[...] = first

    def pack_small():
        value = small[...]
        high = value.astype(BF16).astype(F32)
        low = jnp.broadcast_to((value - high)[V + 1:V + 2], (VP, H))
        small_send[...] = jnp.where(row == V + 2, low, high).astype(BF16)

    def add_small(*terms):
        total = small[...]
        for term in terms:
            total = total + term.astype(F32)
        low = jnp.broadcast_to(total[V + 2:V + 3], (VP, H))
        small[...] = jnp.where(row == V + 1, total + low, jnp.where(row == V + 2, 0.0, total))

    pack_small()
    copy_sa = remote(small_send, small_a, sa_s, sa_r, (e, partner))
    copy_sa.start()

    half = C // 2
    cols = H // Q
    rows_b = half // E
    scatter_c = rows_b % (16 * Z) == 0
    rows_c = rows_b // Z if scatter_c else rows_b
    theirs = pl.multiple_of((1 - c) * half, half)
    mine = pl.multiple_of(c * half, half)

    def last_part(rows, q):
        at = pl.ds(q * cols, cols)
        return gw[pl.ds(rows, half), at] + dot_nt(feat[pl.ds(rows, half), done:], dpre[at, done:])

    copies_a = []
    for q in range(Q):
        gw_send[q] = last_part(theirs, q).astype(BF16)
        copy = remote(gw_send.at[q], recv_a.at[q], a_s.at[q], a_r.at[q], (e, partner))
        copy.start()
        copies_a.append(copy)

    copy_sa.wait()
    add_small(small_a[...])
    pack_small()
    copies_sb = [remote(small_send, small_b.at[d - 1], sb_s.at[d - 1], sb_r.at[d - 1], (ens_peer(d), s)) for d in range(1, E)]
    for copy in copies_sb:
        copy.start()

    copies_b = []
    for q in range(Q):
        own = last_part(mine, q)
        copies_a[q].wait()
        own = own + recv_a[q].astype(F32)
        sum_a[q] = own
        send_b[q] = own.astype(BF16)
        parts = [
            remote(
                send_b.at[q, pl.ds(pl.multiple_of(ens_peer(d) * rows_b, rows_b), rows_b)],
                recv_b.at[q, d - 1], b_s.at[q, d - 1], b_r.at[q, d - 1], (ens_peer(d), s),
            )
            for d in range(1, E)
        ]
        for copy in parts:
            copy.start()
        copies_b.append(parts)

    node_grad[...] = jnp.zeros_like(node_grad)
    wide = pts // 2

    def spread_back(i):
        at = pl.ds(i * wide, wide)
        df = dot(w_in[...], dpre[:, at]).astype(BF16)
        node_grad[...] += dot_nt(table[pl.ds(0, table_len), at], df)

    spread_back(0)
    for copy in copies_sb:
        copy.wait()
    add_small(*[small_b[d - 1] for d in range(1, E)])
    pack_small()
    copies_sc = [remote(small_send, small_c.at[d - 1], sc_s.at[d - 1], sc_r.at[d - 1], (e, 2 * z_peer(d) + c)) for d in range(1, Z)]
    for copy in copies_sc:
        copy.start()

    def stage_c(q):
        for copy in copies_b[q]:
            copy.wait()
        total = sum_a[q, pl.ds(pl.multiple_of(e * rows_b, rows_b), rows_b)]
        for d in range(1, E):
            total = total + recv_b[q, d - 1].astype(F32)
        sum_b[q] = total
        send_c[q] = total.astype(BF16)
        parts = []
        for d in range(1, Z):
            if scatter_c:
                src = send_c.at[q, pl.ds(pl.multiple_of(z_peer(d) * rows_c, rows_c), rows_c)]
            else:
                src = send_c.at[q]
            parts.append(remote(src, recv_c.at[q, d - 1], c_s.at[q, d - 1], c_r.at[q, d - 1], (e, 2 * z_peer(d) + c)))
        for copy in parts:
            copy.start()
        return parts

    copies_c = [stage_c(0)]
    spread_back(1)
    for q in range(1, Q):
        copies_c.append(stage_c(q))

    rim_send[0] = node_grad[pl.ds(R + nodes, R)].astype(BF16)
    rim_send[1] = node_grad[pl.ds(0, R)].astype(BF16)
    rim_up = remote(rim_send.at[0], rim_recv.at[0], rim_s.at[0], rim_r.at[0], (e, s + 1))
    rim_down = remote(rim_send.at[1], rim_recv.at[1], rim_s.at[1], rim_r.at[1], (e, s - 1))

    @pl.when(s < S - 1)
    def _():
        rim_up.start()

    @pl.when(s > 0)
    def _():
        rim_down.start()

    base_b = pl.multiple_of(c * half + e * rows_b, rows_b)
    base_c = pl.multiple_of(base_b + z * rows_c, rows_c) if scatter_c else base_b
    copies_gc = []
    for q in range(Q):
        for copy in copies_c[q]:
            copy.wait()
        if scatter_c:
            total = sum_b[q, pl.ds(pl.multiple_of(z * rows_c, rows_c), rows_c)]
        else:
            total = sum_b[q]
        for d in range(1, Z):
            total = total + recv_c[q, d - 1].astype(F32)
        gout[q, pl.ds(base_c, rows_c)] = total.astype(BF16)
        parts = []
        if scatter_c:
            piece = gout.at[q, pl.ds(base_c, rows_c)]
            parts = [remote(piece, piece, gc_s.at[q, d - 1], gc_r.at[q, d - 1], (e, 2 * z_peer(d) + c)) for d in range(1, Z)]
            for copy in parts:
                copy.start()
        copies_gc.append(parts)

    def to_partner(q, d):
        at = pl.multiple_of(c * half + lax.rem(e + E - d, E) * rows_b, rows_b)
        piece = gout.at[q, pl.ds(at, rows_b)]
        return remote(piece, piece, ga_s.at[q, d], ga_r.at[q, d], (e, partner))

    copies_gb = []
    for q in range(Q):
        for copy in copies_gc[q]:
            copy.wait()
        piece = gout.at[q, pl.ds(base_b, rows_b)]
        parts = [remote(piece, piece, gb_s.at[q, d - 1], gb_r.at[q, d - 1], (ens_peer(d), s)) for d in range(1, E)]
        for copy in parts:
            copy.start()
        to_partner(q, 0).start()
        copies_gb.append(parts)

    @pl.when(s > 0)
    def _():
        rim_up.wait_recv()
        node_grad[pl.ds(R, R)] += rim_recv[0].astype(F32)
        rim_down.wait_send()
        down.wait_send()

    @pl.when(s < S - 1)
    def _():
        rim_down.wait_recv()
        node_grad[pl.ds(nodes, R)] += rim_recv[1].astype(F32)
        rim_up.wait_send()
        up.wait_send()

    stores = [pltpu.make_async_copy(node_grad.at[pl.ds(R, nodes)], node_hbm, out_sem.at[0])]
    stores[0].start()
    for copy in copies_sc:
        copy.wait()
    add_small(*[small_c[d - 1] for d in range(1, Z)])
    stores.append(pltpu.make_async_copy(small, small_hbm, out_sem.at[1]))
    stores[1].start()

    def drain(i, carry):
        for d in range(1, E):
            fc_copy(i, d).wait_send()
        return carry

    lax.fori_loop(0, tiles, drain, 0)
    for q in range(Q):
        for d in range(1, E):
            copies_gb[q][d - 1].wait_recv()
            to_partner(q, d).start()
    for q in range(Q):
        for copy in copies_gb[q]:
            copy.wait_send()
        for d in range(E):
            to_partner(q, d).wait()
    stores.append(pltpu.make_async_copy(gout, gw_hbm, out_sem.at[2]))
    stores[2].start()
    for store in stores:
        store.wait()


def finish(
    scale, loss_scale, V, lane,
    node_in, gw_in, small_in, loss_hbm, node_hbm, gw_hbm, b_in_hbm, w_out_hbm, b_out_hbm,
    node, gw, small, loss, gw_f, b_in, w_out, b_out, sems,
):
    Q, _, cols = gw.shape
    loads = [pltpu.make_async_copy(gw_in.at[q], gw.at[q], sems.at[q]) for q in range(Q)]
    loads.append(pltpu.make_async_copy(small_in, small, sems.at[Q]))
    loads.append(pltpu.make_async_copy(node_in, node, sems.at[Q + 1]))
    for load in loads:
        load.start()
    copies = []
    for q in range(Q):
        loads[q].wait()
        at = pl.ds(q * cols, cols)
        gw_f[:, at] = gw[q].astype(F32) * scale
        copies.append(pltpu.make_async_copy(gw_f.at[:, at], gw_hbm.at[:, at], sems.at[Q + 2 + q]))
        copies[-1].start()
    loads[Q + 1].wait()
    copies.append(pltpu.make_async_copy(node, node_hbm, sems.at[2 * Q + 2]))
    copies[-1].start()
    loads[Q].wait()
    loss[...] = small[V + 1:V + 2, lane:lane + 1] * loss_scale
    b_in[...] = small[V:V + 1, :] * scale
    w_out[...] = small[:V, :] * scale
    b_out[...] = small[V + 1:V + 2, :V] * scale
    for i, (src, dst) in enumerate(((loss, loss_hbm), (b_in, b_in_hbm), (w_out, w_out_hbm), (b_out, b_out_hbm))):
        copies.append(pltpu.make_async_copy(src, dst, sems.at[2 * Q + 3 + i]))
        copies[-1].start()
    for copy in copies:
        copy.wait()


def per_device(
    node_latent, point_skip, edge_index, edge_weight, w_in, b_in, readout_matrix, output_bias, truth
):
    members, nodes, C = node_latent.shape
    assert members == 1
    pts = point_skip.shape[0]
    H = w_in.shape[1]
    V = truth.shape[0]
    E = lax.axis_size("ens")
    S = lax.axis_size("space")
    Z = S // 2
    R = nodes // 8
    VP = 16
    Q = 2
    cols = H // Q
    K = edge_index.shape[0]
    T = min(512, pts // 2)
    tiles = pts // T
    table_len = nodes + 2 * R
    half = C // 2
    rows_b = half // E
    rows_c = rows_b // Z if rows_b % (16 * Z) == 0 else rows_b
    hbm = pl.BlockSpec(memory_space=pltpu.HBM)
    dma = pltpu.SemaphoreType.DMA
    node_grad, gw, small = pl.pallas_call(
        functools.partial(kernel, (E, S, T, R, Q)),
        out_shape=(
            jax.ShapeDtypeStruct((nodes, C), F32),
            jax.ShapeDtypeStruct((Q, C, cols), BF16),
            jax.ShapeDtypeStruct((VP, H), F32),
        ),
        in_specs=[hbm] * 9,
        out_specs=(hbm, hbm, hbm),
        scratch_shapes=[
            pltpu.VMEM((nodes, C), BF16),
            pltpu.VMEM((pts, C), BF16),
            pltpu.VMEM((K, pts), jnp.int32),
            pltpu.VMEM((K, pts), F32),
            pltpu.VMEM((C, H), BF16),
            pltpu.VMEM((1, H), F32),
            pltpu.VMEM((V, H), BF16),
            pltpu.VMEM((1, V), F32),
            pltpu.VMEM((V, pts), F32),
            pltpu.VMEM((2 * table_len, C), BF16),
            pltpu.VMEM((C, 2 * table_len), BF16),
            pltpu.VMEM((2 * table_len, pts), BF16),
            pltpu.VMEM((H, C), BF16),
            pltpu.VMEM((C, pts), BF16),
            pltpu.VMEM((H, pts), BF16),
            pltpu.VMEM((H, pts), F32),
            pltpu.VMEM((H, pts), BF16),
            pltpu.VMEM((tiles, V, T), F32),
            pltpu.VMEM((tiles, E - 1, V, T), F32),
            pltpu.VMEM((VP, H), F32),
            pltpu.VMEM((VP, pts), F32),
            pltpu.VMEM((H, 128), F32),
            pltpu.VMEM((H, 128), F32),
            pltpu.VMEM((VP, T), F32),
            pltpu.VMEM((VP, T), F32),
            pltpu.VMEM((table_len, C), F32),
            pltpu.VMEM((2, R, C), BF16),
            pltpu.VMEM((2, R, C), BF16),
            pltpu.VMEM((C, H), F32),
            pltpu.VMEM((Q, half, cols), BF16),
            pltpu.VMEM((Q, half, cols), F32),
            pltpu.VMEM((Q, half, cols), BF16),
            pltpu.VMEM((Q, half, cols), BF16),
            pltpu.VMEM((Q, rows_b, cols), F32),
            pltpu.VMEM((Q, E - 1, rows_b, cols), BF16),
            pltpu.VMEM((Q, rows_b, cols), BF16),
            pltpu.VMEM((Q, Z - 1, rows_c, cols), BF16),
            pltpu.VMEM((Q, C, cols), BF16),
            pltpu.VMEM((VP, H), F32),
            pltpu.VMEM((VP, H), BF16),
            pltpu.VMEM((VP, H), BF16),
            pltpu.VMEM((E - 1, VP, H), BF16),
            pltpu.VMEM((Z - 1, VP, H), BF16),
            dma((9,)), dma((3,)), dma((2,)), dma((2,)),
            dma((tiles, E - 1)), dma((tiles, E - 1)),
            dma((2,)), dma((2,)),
            dma((Q,)), dma((Q,)),
            dma((Q, E - 1)), dma((Q, E - 1)),
            dma((Q, Z - 1)), dma((Q, Z - 1)),
            dma((Q, Z - 1)), dma((Q, Z - 1)),
            dma((Q, E - 1)), dma((Q, E - 1)),
            dma((Q, E)), dma((Q, E)),
            dma, dma,
            dma((E - 1,)), dma((E - 1,)),
            dma((Z - 1,)), dma((Z - 1,)),
        ],
        compiler_params=pltpu.CompilerParams(
            collective_id=0, has_side_effects=True, vmem_limit_bytes=62 * 2**20
        ),
        cost_estimate=pl.CostEstimate(flops=8 * 10**9, bytes_accessed=5 * 10**6, transcendentals=2 * 10**6),
    )(
        node_latent[0], point_skip, edge_index, edge_weight, w_in, b_in[None], readout_matrix,
        output_bias[None], truth,
    )
    points = pts * S
    scale = 1.0 / math.sqrt(E * points)
    sds = jax.ShapeDtypeStruct
    loss, node_grad, gw, gb_in, gw_out, gb_out = pl.pallas_call(
        functools.partial(finish, scale, 1.0 / (points * V), V, VP),
        out_shape=(
            sds((1, 1), F32), sds((nodes, C), F32), sds((C, H), F32),
            sds((1, H), F32), sds((V, H), F32), sds((1, V), F32),
        ),
        in_specs=[hbm] * 3,
        out_specs=(hbm,) * 6,
        scratch_shapes=[
            pltpu.VMEM((nodes, C), F32), pltpu.VMEM((Q, C, cols), BF16), pltpu.VMEM((VP, H), F32),
            pltpu.VMEM((1, 1), F32), pltpu.VMEM((C, H), F32), pltpu.VMEM((1, H), F32),
            pltpu.VMEM((V, H), F32), pltpu.VMEM((1, V), F32), dma((2 * Q + 7,)),
        ],
        compiler_params=pltpu.CompilerParams(vmem_limit_bytes=62 * 2**20),
    )(node_grad, gw, small)
    return loss[0, 0], node_grad[None], gw, gb_in[0], gw_out, gb_out[0]


def solution(mesh):
    return jax.shard_map(
        per_device,
        mesh=mesh,
        in_specs=(
            P("ens", "space", None), P("space", None), P(None, "space"), P(None, "space"),
            P(), P(), P(), P(), P(None, "space"),
        ),
        out_specs=(P(), P("ens", "space", None), P(), P(), P(), P()),
        check_vma=False,
    )
```
